32 devices in a mesh: groups: 2 (over y), sector: 4 (over z), term: 2 (over x), rep: 2 (over core).
Axes of the slice: x: 2, y: 2, z: 4, core: 2. Of those that a mesh axis runs over, the one named last changes fastest.
Arguments:
- start_vector: bfloat16 [8, 4, 256, 256], P(('groups', 'sector'), None, None, 'rep'), parts along dimension 0, may hold values from -3600 to 3600
- precond: bfloat16 [8, 4, 256, 256], P(('groups', 'sector'), None, None, 'rep'), parts along dimension 0, may hold values from 0.5 to 4
- left_env: bfloat16 [2, 8, 4, 256, 256], P('term', ('groups', 'sector')), parts along dimension 1, may hold values from -6 to 6, as said below
- right_env: bfloat16 [2, 4, 8, 256, 256], P('term', 'sector', 'groups', None, 'rep'), parts along dimension 2, may hold values from -6 to 6, as said below
- blocks_used: int32 [2, 8, 4], P('term', ('groups', 'sector')), parts along dimension 1, may hold values 0 or 1
Outputs:
- next_vector: float32 [8, 4, 256, 256], P(('groups', 'sector'), None, None, 'rep'), parts along dimension 0
- next_image: float32 [8, 4, 256, 256], P(('groups', 'sector'), None, None, 'rep'), parts along dimension 0
- ritz_value: float32 [2], P('groups'), parts along dimension 0
The draws below stay inside these ranges and needn't reach their ends.
There are 2 independent parts, one for each index of `groups`. The reference program is written for one: setup_inputs(seed, part) draws one part's arguments, and reference() takes and returns one part's arrays. A program takes and returns all parts, laid end to end along the dimension named above; each array names one. Nothing has to cross between parts.
Inputs may be any that keep to these rules, and one draw needn't show every extreme that they name: `left_env`: each block of every term is symmetric in its two bond indices. `right_env`: each block of every term is symmetric in its two bond indices.
All inputs are finite; a program needn't handle non-finite values. No bound on the sum of `blocks_used` on one device may be relied on, other than what follows from the above.
Results may differ from the reference program's by a relative error of at most 0.0029.
The reference program's roundings to bfloat16 on the way count: a program that leaves them out, or rounds other values in their place, can miss the bound.
Values may be sent and summed in bfloat16 or wider, within the bound.
A program may use at most 64 MiB of HBM per device.

```python
import math
import jax
import jax.numpy as jnp
from jax import lax

BLOCK = 256
SA = 4
SB = 4
TERMS = 2


def symmetrize(base, scale):
    return (base + jnp.swapaxes(base, -1, -2)) * (scale / math.sqrt(2.0))


def draw_left_env(key, part):
    key = jax.random.fold_in(key, 11)
    shape = (TERMS, SA, SB, BLOCK, BLOCK)
    base = jnp.clip(jax.random.normal(key, shape, jnp.float32), -4.0, 4.0)
    return symmetrize(base, 1.0 / math.sqrt(BLOCK * TERMS)).astype(jnp.bfloat16)


def draw_right_env(key, part):
    key = jax.random.fold_in(key, 13)
    shape = (TERMS, SB, SA, BLOCK, BLOCK)
    base = jnp.clip(jax.random.normal(key, shape, jnp.float32), -4.0, 4.0)
    return symmetrize(base, 1.0 / math.sqrt(BLOCK)).astype(jnp.bfloat16)


def draw_start_vector(key, part):
    key = jax.random.fold_in(key, 17)
    key_base, key_rows, key_cols = jax.random.split(key, 3)
    shape = (SA, SB, BLOCK, BLOCK)
    base = jnp.clip(jax.random.normal(key_base, shape, jnp.float32), -4.0, 4.0)
    rows = jnp.exp(jax.random.uniform(key_rows, (SA, SB, BLOCK, 1), jnp.float32, 0.0, math.log(10.0)))
    cols = jnp.exp(jax.random.uniform(key_cols, (SA, SB, 1, BLOCK), jnp.float32, 0.0, math.log(10.0)))
    ramp = 1.0 + 2.0 * jnp.arange(SA, dtype=jnp.float32) / (SA - 1)
    ramp = jnp.reshape(ramp, (SA, 1, 1, 1))
    return (base * rows * cols * ramp).astype(jnp.bfloat16)


def plant(drawn, rng, low, high):
    place = [jax.random.randint(jax.random.fold_in(rng, axis), (), 0, length) for axis, length in enumerate(drawn.shape)]
    widest = drawn.shape.index(max(drawn.shape))
    neighbour = place[:widest] + [(place[widest] + 1) % drawn.shape[widest]] + place[widest + 1:]
    return drawn.at[tuple(place)].set(low).at[tuple(neighbour)].set(high)


def shard_levels(rng, extent, cuts, least, largest):
    def one(dim, parts):
        heights = jax.random.uniform(jax.random.fold_in(jax.random.fold_in(rng, 6), dim), (parts,), jnp.float32, least / len(cuts), largest / len(cuts))
        return jnp.repeat(jnp.exp(heights), extent[dim] // parts).reshape((-1,) + (1,) * (len(extent) - dim - 1))

    factor_of = one(*cuts[0])
    for cut in cuts[1:]:
        factor_of = factor_of * one(*cut)
    return factor_of


def setup_inputs(seed: int = 0, part: int = 0) -> dict:
    key_of = jax.random.split(jax.random.key(seed), 6)
    own_keys = jax.random.split(jax.random.fold_in(key_of[5], part), 6)
    start_vector = draw_start_vector(jax.random.fold_in(jax.random.fold_in(key_of[5], part), 71), part)
    precond = jnp.clip(jnp.exp(math.log(4.0) - 2.0794415 * jax.random.uniform(own_keys[1], (SA, SB, BLOCK, BLOCK), jnp.float32) ** shard_levels(own_keys[1], (SA, SB, BLOCK, BLOCK), ((0, 4), (3, 2)), -0.2, 0.2)), 0.5, 4.0).astype(jnp.bfloat16)
    left_env = draw_left_env(jax.random.fold_in(jax.random.fold_in(key_of[5], part), 71), part)
    right_env = draw_right_env(jax.random.fold_in(jax.random.fold_in(key_of[5], part), 71), part)
    blocks_used = plant((jax.random.randint(own_keys[4], (TERMS, SA, SB), 0, 4) < 3).astype(jnp.int32), jax.random.fold_in(own_keys[4], 1), 0, 1)
    return dict(start_vector=start_vector, precond=precond, left_env=left_env, right_env=right_env, blocks_used=blocks_used)


eps = 1e-06

def apply_h(vector, left_env, right_env, blocks_used):
    rounded = lax.optimization_barrier(vector.astype(jnp.bfloat16)).astype(jnp.float32)

    def one_term(total, pieces):
        left_t, right_t, used_t = pieces
        mixed = jnp.einsum('ijab,ijbc->ijac', left_t.astype(jnp.float32), rounded)
        mixed = mixed * used_t[:, :, None, None].astype(jnp.float32)
        mixed = lax.optimization_barrier(mixed.astype(jnp.bfloat16)).astype(jnp.float32)
        return (total + jnp.einsum('ijac,jidc->ijad', mixed, right_t.astype(jnp.float32)), None)
    start = jnp.zeros(vector.shape, jnp.float32)
    total, _ = lax.scan(one_term, start, (left_env, right_env, blocks_used))
    return total

def orthonormal(target, bases):
    count = target.size
    rest = target
    coefs = [jnp.sum(basis * target) / count for basis in bases]
    for basis, coef in zip(bases, coefs):
        rest = rest - coef * basis
    length = jnp.sum(rest * rest) / count
    return rest / jnp.sqrt(length + eps)

def reference(start_vector, precond, left_env, right_env, blocks_used):
    vector = start_vector.astype(jnp.float32)
    count = vector.size
    vzero = vector / jnp.sqrt(jnp.sum(vector * vector) / count + eps)
    scaling = precond.astype(jnp.float32)
    sigma_zero = apply_h(vzero, left_env, right_env, blocks_used)
    theta = jnp.sum(vzero * sigma_zero) / count
    vone = orthonormal((sigma_zero - theta * vzero) / scaling, (vzero,))
    sigma_one = apply_h(vone, left_env, right_env, blocks_used)
    cross = jnp.sum(vone * sigma_zero) / count
    diag_one = jnp.sum(vone * sigma_one) / count
    half_gap = (theta - diag_one) * 0.5
    lowest = (theta + diag_one) * 0.5 - jnp.sqrt(half_gap * half_gap + cross * cross)
    length = jnp.sqrt(cross * cross + (lowest - theta) * (lowest - theta))
    coef_zero = cross / length
    coef_one = (lowest - theta) / length
    residual_one = coef_zero * sigma_zero + coef_one * sigma_one - lowest * (coef_zero * vzero + coef_one * vone)
    vtwo = orthonormal(residual_one / scaling, (vzero, vone))
    sigma_two = apply_h(vtwo, left_env, right_env, blocks_used)
    return (vtwo, sigma_two, jnp.reshape(lowest, (1,)))
```

```python
import functools
import jax
import jax.numpy as jnp
from jax import lax
from jax.experimental import pallas as pl
from jax.experimental.pallas import tpu as pltpu
from jax.sharding import PartitionSpec as P

eps = 1e-06
MESH = pl.DeviceIdType.MESH
f32 = jnp.float32
bf16 = jnp.bfloat16


def loop(low, high, body):
    if high - low <= 16:
        for k in range(low, high):
            body(k)
    else:
        lax.fori_loop(low, high, lambda k, c: (body(k), c)[1], 0)


def pack(sums):
    lane = lax.broadcasted_iota(jnp.int32, (1, 128), 1)
    row = jnp.zeros((1, 128), f32)
    for k, value in enumerate(sums):
        if value.shape != (1, 1):
            value = jnp.sum(value, axis=1, keepdims=True)
        row = row + jnp.where(lane == k, value, 0.0)
    return row


def partial(products):
    total = products[0]
    for other in products[1:]:
        total = total + other
    return jnp.sum(total, axis=0, keepdims=True)


def kernel(
    S, T, R, nj, count,
    v_in, p_in, l_in, r_in, used,
    nv_out, img_out, ritz_out,
    vloc, vbuf, pbuf, lbuf, rbuf, nvbuf, imgbuf, rows,
    local_sem, vsem, psem, lsem, rsem, row_sem, row_send, v_send, p_send, l_send, r_send,
    out_sem, out_send,
):
    N = S * T * R
    SB = nj * T * R
    B = lbuf.shape[-1]
    H = B // R
    s, t, r = lax.axis_index("sector"), lax.axis_index("term"), lax.axis_index("rep")
    me = (s * T + t) * R + r

    def device(rank):
        return {"sector": rank // (T * R), "term": lax.rem(rank // R, T), "rep": lax.rem(rank, R)}

    def first(t2, r2):
        return (t2 * R + r2) * nj

    def half(r2):
        return pl.ds(pl.multiple_of(r2 * H, H), H)

    own = pl.ds(first(t, r), nj)
    load = pltpu.make_async_copy(v_in.at[0, pl.ds(t * R * nj, R * nj)], vloc, local_sem)
    load.start()
    pltpu.make_async_copy(v_in.at[0, own], vbuf.at[:, :, half(r)], vsem).start()
    pltpu.make_async_copy(p_in.at[0, own], pbuf.at[:, :, half(r)], psem).start()
    pltpu.make_async_copy(l_in.at[0, 0, own], lbuf.at[t], lsem).start()

    barrier = pltpu.get_barrier_semaphore()

    def greet(k):
        pl.semaphore_signal(barrier, inc=1, device_id=device(lax.rem(me + k, N)), device_id_type=MESH)

    loop(1, N, greet)

    load.wait()
    lane = lax.broadcasted_iota(jnp.int32, (1, 128), 1)
    local_v = [vloc[k].astype(f32) for k in range(R * nj)]
    row = pack([partial([x * x for x in local_v])])
    for j in range(SB):
        row = row + jnp.where(lane == 8 + j, used[0, 0, j].astype(f32), 0.0)

    def send_row(index, row):
        rows[index, me] = row

        def one(k):
            peer = lax.rem(me + k, N)
            pltpu.make_async_remote_copy(
                rows.at[index, me], rows.at[index, me], row_send.at[index], row_sem.at[index],
                device_id=device(peer), device_id_type=MESH,
            ).start()

        loop(1, N, one)

    def wait_rows(index):
        some = rows.at[index, pl.ds(0, N - 1)]
        pltpu.make_async_copy(some, some, row_sem.at[index]).wait()
        return rows[index].reshape(N, 128)

    pl.semaphore_wait(barrier, N - 1)
    send_row(0, row)

    def v_copy(k, src, dst, sem, recv):
        r2 = lax.rem(r + k, R)
        return pltpu.make_async_remote_copy(
            src.at[0, pl.ds(first(t, r2), nj)], dst.at[:, :, half(r)], sem.at[k - 1], recv,
            device_id={"sector": s, "term": t, "rep": r2}, device_id_type=MESH,
        )

    def l_copy(k):
        t2 = lax.rem(t + k, T)
        return pltpu.make_async_remote_copy(
            l_in.at[0, 0, pl.ds(first(t2, r), nj)], lbuf.at[t], l_send.at[k - 1], lsem,
            device_id={"sector": s, "term": t2, "rep": r}, device_id_type=MESH,
        )

    owner = s // nj
    owner_t, owner_r, slot = owner // R, lax.rem(owner, R), lax.rem(s, nj)
    mine = jnp.logical_and(owner_t == t, owner_r == r)

    def r_copy(k):
        i2 = lax.rem(s + k, S)
        return pltpu.make_async_remote_copy(
            r_in.at[0, 0, i2], rbuf.at[t, slot, :, half(r)], r_send.at[k], rsem,
            device_id={"sector": i2, "term": owner_t, "rep": owner_r}, device_id_type=MESH,
        )

    loop(1, R, lambda k: v_copy(k, v_in, vbuf, v_send, vsem).start())
    loop(1, R, lambda k: v_copy(k, p_in, pbuf, p_send, psem).start())
    loop(1, S, lambda k: r_copy(k).start())

    @pl.when(mine)
    def _():
        pltpu.make_async_copy(r_in.at[0, 0, s], rbuf.at[t, slot, :, half(r)], rsem).start()

    @pl.when(jnp.logical_not(mine))
    def _():
        r_copy(0).start()

    loop(1, T, lambda k: l_copy(k).start())

    def whole(ref, sem):
        pltpu.make_async_copy(ref, ref, sem).wait()

    m0 = wait_rows(0)
    square = jnp.sum(m0[:, 0:1], axis=0, keepdims=True) / count
    scale = 1.0 / jnp.sqrt(square + eps)
    masks = []
    for t2 in range(T):
        peer_row = rows[0, (s * T + t2) * R + r]
        masks.append([
            jnp.sum(jnp.where(lane == 8 + first(t, r) + q, peer_row, 0.0), axis=1, keepdims=True)
            for q in range(nj)
        ])
    whole(vbuf, vsem)
    v0 = [vbuf[q].astype(f32) * scale for q in range(nj)]
    whole(pbuf, psem)
    ip = [1.0 / pbuf[q].astype(f32) for q in range(nj)]
    whole(lbuf, lsem)
    whole(rbuf, rsem)

    def apply_h(v):
        result = []
        for q in range(nj):
            rounded = v[q].astype(bf16)
            total = None
            for t2 in range(T):
                mixed = jnp.dot(lbuf[t2, q], rounded, preferred_element_type=f32)
                mixed = (mixed * masks[t2][q]).astype(bf16)
                piece = lax.dot_general(
                    mixed, rbuf[t2, q], (((1,), (1,)), ((), ())), preferred_element_type=f32
                )
                total = piece if total is None else total + piece
            result.append(total)
        return result

    def inner(x, y):
        return partial([a * b for a, b in zip(x, y)])

    def lanes(x):
        return jnp.sum(x, axis=1, keepdims=True)

    def columns(m, n):
        return [m[:, k:k + 1] for k in range(n)]

    def add(x):
        return jnp.sum(x, axis=0, keepdims=True) / count

    s0 = apply_h(v0)
    n_loc = lanes(inner(v0, v0))
    a_loc = lanes(inner(v0, s0))
    th_loc = a_loc / jnp.maximum(n_loc, 1e-30)
    bb = [a * b for a, b in zip(v0, ip)]
    tt = [(a - th_loc * b) * c for a, b, c in zip(s0, v0, ip)]
    send_row(1, pack([
        n_loc, a_loc, th_loc, inner(v0, tt), inner(v0, bb), inner(tt, tt), inner(tt, bb),
        inner(bb, bb), inner(tt, s0), inner(bb, s0),
    ]))
    n0, a0, th, vt, vb, t_t, t_b, b_b, ts, bs = columns(wait_rows(1), 10)
    theta = add(a0)
    delta = th - theta
    coef = add(vt + delta * vb)
    length = add(
        t_t + delta * (2.0 * t_b + delta * b_b) - coef * (2.0 * (vt + delta * vb) - coef * n0)
    )
    inv = 1.0 / jnp.sqrt(jnp.maximum(length, 0.0) + eps)
    cross = add(ts + delta * bs - coef * a0) * inv
    d_loc = th_loc - theta
    v1 = [(x + d_loc * y - coef * z) * inv for x, y, z in zip(tt, bb, v0)]

    s1 = apply_h(v1)
    xx = [(x - theta * y - cross * z) * w for x, y, z, w in zip(s0, v0, v1, ip)]
    zz = [x * y for x, y in zip(v1, ip)]
    n1_loc = lanes(inner(v1, v1))
    d1_loc = lanes(inner(v1, s1))
    g_loc = d1_loc / jnp.maximum(n1_loc, 1e-30)
    yy = [(x - cross * y - g_loc * z) * w for x, y, z, w in zip(s1, v0, v1, ip)]
    send_row(2, pack([
        n1_loc, d1_loc, g_loc, inner(v0, v1),
        inner(xx, xx), inner(xx, yy), inner(xx, zz), inner(yy, yy), inner(yy, zz), inner(zz, zz),
        inner(v0, xx), inner(v0, yy), inner(v0, zz), inner(v1, xx), inner(v1, yy), inner(v1, zz),
    ]))
    (n1, d1, g, o01, xx_, xy_, xz_, yy_, yz_, zz_, ax, ay, az, bx, by, bz) = columns(wait_rows(2), 16)
    diag = add(d1)
    gap = (theta - diag) * 0.5
    lowest = (theta + diag) * 0.5 - jnp.sqrt(gap * gap + cross * cross)
    size = jnp.sqrt(cross * cross + (lowest - theta) * (lowest - theta))
    c0 = cross / size
    c1 = (lowest - theta) / size
    e = c1 * (g - diag)
    f0d = c0 * ax + c1 * ay + e * az
    f1d = c0 * bx + c1 * by + e * bz
    f0 = add(f0d)
    f1 = add(f1d)
    square1 = (
        c0 * c0 * xx_ + c1 * c1 * yy_ + e * e * zz_
        + 2.0 * (c0 * c1 * xy_ + c0 * e * xz_ + c1 * e * yz_)
    )
    length1 = add(
        square1 - 2.0 * (f0 * f0d + f1 * f1d) + f0 * f0 * n0 + f1 * f1 * n1 + 2.0 * f0 * f1 * o01
    )
    inv1 = 1.0 / jnp.sqrt(jnp.maximum(length1, 0.0) + eps)
    e_loc = c1 * (g_loc - diag)
    v2 = []
    for q in range(nj):
        new = (c0 * xx[q] + c1 * yy[q] + e_loc * zz[q] - f0 * v0[q] - f1 * v1[q]) * inv1
        nvbuf[q] = new
        v2.append(new)

    def out_copy(k, src, dst, which):
        place = lax.rem(t * R + r + k, T * R)
        t2, r2 = place // R, lax.rem(place, R)
        if k == 0:
            return pltpu.make_async_copy(src.at[:, :, half(r2)], dst.at[0, own], out_sem.at[which])
        return pltpu.make_async_remote_copy(
            src.at[:, :, half(r2)], dst.at[0, own], out_send.at[which, k - 1], out_sem.at[which],
            device_id={"sector": s, "term": t2, "rep": r2}, device_id_type=MESH,
        )

    for k in range(T * R):
        out_copy(k, nvbuf, nv_out, 0).start()
    s2 = apply_h(v2)
    for q in range(nj):
        imgbuf[q] = s2[q]
    for k in range(T * R):
        out_copy(k, imgbuf, img_out, 1).start()
    ritz_out[0] = jnp.sum(lowest)

    for index in range(3):
        some = rows.at[index, pl.ds(0, N - 1)]
        pltpu.make_async_copy(some, some, row_send.at[index]).wait()
    loop(1, R, lambda k: v_copy(k, v_in, vbuf, v_send, vsem).wait_send())
    loop(1, R, lambda k: v_copy(k, p_in, pbuf, p_send, psem).wait_send())
    loop(1, S, lambda k: r_copy(k).wait_send())

    @pl.when(jnp.logical_not(mine))
    def _():
        r_copy(0).wait_send()

    loop(1, T, lambda k: l_copy(k).wait_send())
    for k in range(1, T * R):
        out_copy(k, nvbuf, nv_out, 0).wait_send()
        out_copy(k, imgbuf, img_out, 1).wait_send()
    whole(nv_out, out_sem.at[0])
    whole(img_out, out_sem.at[1])


def solution(mesh):
    S, T, R = mesh.shape["sector"], mesh.shape["term"], mesh.shape["rep"]

    def local(start_vector, precond, left_env, right_env, blocks_used):
        SB, B, H = start_vector.shape[1:]
        nj = SB // (T * R)
        N = S * T * R
        count = float(start_vector.size * S * R)
        dma = pltpu.SemaphoreType.DMA
        hbm = pl.BlockSpec(memory_space=pl.ANY)
        vmem = pl.BlockSpec(memory_space=pltpu.VMEM)
        smem = pl.BlockSpec(memory_space=pltpu.SMEM)
        shape = jax.ShapeDtypeStruct(start_vector.shape, f32)
        return tuple(pl.pallas_call(
            functools.partial(kernel, S, T, R, nj, count),
            out_shape=(shape, shape, jax.ShapeDtypeStruct((1,), f32)),
            in_specs=[hbm, hbm, hbm, hbm, smem],
            out_specs=(vmem, vmem, smem),
            scratch_shapes=[
                pltpu.VMEM((R * nj, B, H), bf16),
                pltpu.VMEM((nj, B, B), bf16),
                pltpu.VMEM((nj, B, B), bf16),
                pltpu.VMEM((T, nj, B, B), bf16),
                pltpu.VMEM((T, nj, B, B), bf16),
                pltpu.VMEM((nj, B, B), f32),
                pltpu.VMEM((nj, B, B), f32),
                pltpu.VMEM((3, N, 1, 128), f32),
                dma, dma, dma, dma, dma, dma((3,)), dma((3,)), dma((R,)), dma((R,)), dma((T,)),
                dma((S,)), dma((2,)), dma((2, T * R)),
            ],
            compiler_params=pltpu.CompilerParams(
                collective_id=0, has_side_effects=True, vmem_limit_bytes=40 * 2**20
            ),
            name="davidson",
        )(start_vector, precond, left_env, right_env, blocks_used))

    in_specs = (
        P(("groups", "sector"), None, None, "rep"),
        P(("groups", "sector"), None, None, "rep"),
        P("term", ("groups", "sector"), None, None, None),
        P("term", "sector", "groups", None, "rep"),
        P("term", ("groups", "sector"), None),
    )
    out_specs = (
        P(("groups", "sector"), None, None, "rep"),
        P(("groups", "sector"), None, None, "rep"),
        P("groups"),
    )
    return jax.shard_map(local, mesh=mesh, in_specs=in_specs, out_specs=out_specs, check_vma=False)
```

```python
import functools
import jax
import jax.numpy as jnp
from jax import lax
from jax.experimental import pallas as pl
from jax.experimental.pallas import tpu as pltpu
from jax.sharding import PartitionSpec as P

eps = 1e-06
MESH = pl.DeviceIdType.MESH
f32 = jnp.float32
bf16 = jnp.bfloat16


def loop(low, high, body):
    if high - low <= 16:
        for k in range(low, high):
            body(k)
    else:
        lax.fori_loop(low, high, lambda k, c: (body(k), c)[1], 0)


def pack(sums):
    lane = lax.broadcasted_iota(jnp.int32, (1, 128), 1)
    row = jnp.zeros((1, 128), f32)
    for k, value in enumerate(sums):
        if value.shape != (1, 1):
            value = jnp.sum(value, axis=1, keepdims=True)
        row = row + jnp.where(lane == k, value, 0.0)
    return row


def partial(products):
    total = products[0]
    for other in products[1:]:
        total = total + other
    return jnp.sum(total, axis=0, keepdims=True)


def kernel(
    S, T, R, nj, count,
    v_in, p_in, l_in, r_in, used,
    nv_out, img_out, ritz_out,
    vloc, vbuf, pbuf, lbuf, rbuf, nvbuf, imgbuf, rows,
    local_sem, vsem, psem, lsem, rsem, row_sem, row_send, v_send, p_send, l_send, r_send,
    out_sem, out_send,
):
    N = S * T * R
    SB = nj * T * R
    B = lbuf.shape[-1]
    H = B // R
    s, t, r = lax.axis_index("sector"), lax.axis_index("term"), lax.axis_index("rep")
    me = (s * T + t) * R + r

    def device(rank):
        return {"sector": rank // (T * R), "term": lax.rem(rank // R, T), "rep": lax.rem(rank, R)}

    def first(t2, r2):
        return (t2 * R + r2) * nj

    def half(r2):
        return pl.ds(pl.multiple_of(r2 * H, H), H)

    own = pl.ds(first(t, r), nj)
    load = pltpu.make_async_copy(v_in.at[0, pl.ds(t * R * nj, R * nj)], vloc, local_sem)
    load.start()
    pltpu.make_async_copy(v_in.at[0, own], vbuf.at[:, :, half(r)], vsem).start()
    pltpu.make_async_copy(p_in.at[0, own], pbuf.at[:, :, half(r)], psem).start()
    pltpu.make_async_copy(l_in.at[0, 0, own], lbuf.at[t], lsem).start()

    barrier = pltpu.get_barrier_semaphore()

    def greet(k):
        pl.semaphore_signal(barrier, inc=1, device_id=device(lax.rem(me + k, N)), device_id_type=MESH)

    loop(1, N, greet)

    load.wait()
    lane = lax.broadcasted_iota(jnp.int32, (1, 128), 1)
    local_v = [vloc[k].astype(f32) for k in range(R * nj)]
    row = pack([partial([x * x for x in local_v])])
    for j in range(SB):
        row = row + jnp.where(lane == 8 + j, used[0, 0, j].astype(f32), 0.0)

    def send_row(index, row):
        rows[index, me] = row

        def one(k):
            peer = lax.rem(me + k, N)
            pltpu.make_async_remote_copy(
                rows.at[index, me], rows.at[index, me], row_send.at[index], row_sem.at[index],
                device_id=device(peer), device_id_type=MESH,
            ).start()

        loop(1, N, one)

    def wait_rows(index):
        some = rows.at[index, pl.ds(0, N - 1)]
        pltpu.make_async_copy(some, some, row_sem.at[index]).wait()
        return rows[index].reshape(N, 128)

    pl.semaphore_wait(barrier, N - 1)
    send_row(0, row)

    def v_copy(k, src, dst, sem, recv):
        r2 = lax.rem(r + k, R)
        return pltpu.make_async_remote_copy(
            src.at[0, pl.ds(first(t, r2), nj)], dst.at[:, :, half(r)], sem.at[k - 1], recv,
            device_id={"sector": s, "term": t, "rep": r2}, device_id_type=MESH,
        )

    def l_copy(k):
        t2 = lax.rem(t + k, T)
        return pltpu.make_async_remote_copy(
            l_in.at[0, 0, pl.ds(first(t2, r), nj)], lbuf.at[t], l_send.at[k - 1], lsem,
            device_id={"sector": s, "term": t2, "rep": r}, device_id_type=MESH,
        )

    owner = s // nj
    owner_t, owner_r, slot = owner // R, lax.rem(owner, R), lax.rem(s, nj)
    mine = jnp.logical_and(owner_t == t, owner_r == r)

    def r_copy(k):
        i2 = lax.rem(s + k, S)
        return pltpu.make_async_remote_copy(
            r_in.at[0, 0, i2], rbuf.at[t, slot, :, half(r)], r_send.at[k], rsem,
            device_id={"sector": i2, "term": owner_t, "rep": owner_r}, device_id_type=MESH,
        )

    loop(1, R, lambda k: v_copy(k, v_in, vbuf, v_send, vsem).start())
    loop(1, R, lambda k: v_copy(k, p_in, pbuf, p_send, psem).start())
    loop(1, S, lambda k: r_copy(k).start())

    @pl.when(mine)
    def _():
        pltpu.make_async_copy(r_in.at[0, 0, s], rbuf.at[t, slot, :, half(r)], rsem).start()

    @pl.when(jnp.logical_not(mine))
    def _():
        r_copy(0).start()

    loop(1, T, lambda k: l_copy(k).start())

    def whole(ref, sem):
        pltpu.make_async_copy(ref, ref, sem).wait()

    m0 = wait_rows(0)
    square = jnp.sum(m0[:, 0:1], axis=0, keepdims=True) / count
    scale = 1.0 / jnp.sqrt(square + eps)
    masks = []
    for t2 in range(T):
        peer_row = rows[0, (s * T + t2) * R + r]
        masks.append([
            jnp.sum(jnp.where(lane == 8 + first(t, r) + q, peer_row, 0.0), axis=1, keepdims=True)
            for q in range(nj)
        ])
    whole(vbuf, vsem)
    v0 = [vbuf[q].astype(f32) * scale for q in range(nj)]
    whole(pbuf, psem)
    ip = [1.0 / pbuf[q].astype(f32) for q in range(nj)]
    whole(lbuf, lsem)
    whole(rbuf, rsem)

    def apply_h(v):
        result = []
        for q in range(nj):
            rounded = v[q].astype(bf16)
            total = None
            for t2 in range(T):
                mixed = jnp.dot(lbuf[t2, q], rounded, preferred_element_type=f32)
                mixed = (mixed * masks[t2][q]).astype(bf16)
                piece = lax.dot_general(
                    mixed, rbuf[t2, q], (((1,), (1,)), ((), ())), preferred_element_type=f32
                )
                total = piece if total is None else total + piece
            result.append(total)
        return result

    def inner(x, y):
        return partial([a * b for a, b in zip(x, y)])

    def lanes(x):
        return jnp.sum(x, axis=1, keepdims=True)

    def columns(m, n):
        return [m[:, k:k + 1] for k in range(n)]

    def add(x):
        return jnp.sum(x, axis=0, keepdims=True) / count

    s0 = apply_h(v0)
    n_loc = lanes(inner(v0, v0))
    a_loc = lanes(inner(v0, s0))
    th_loc = a_loc / jnp.maximum(n_loc, 1e-30)
    bb = [a * b for a, b in zip(v0, ip)]
    tt = [(a - th_loc * b) * c for a, b, c in zip(s0, v0, ip)]
    send_row(1, pack([
        n_loc, a_loc, th_loc, inner(v0, tt), inner(v0, bb), inner(tt, tt), inner(tt, bb),
        inner(bb, bb), inner(tt, s0), inner(bb, s0),
    ]))
    n0, a0, th, vt, vb, t_t, t_b, b_b, ts, bs = columns(wait_rows(1), 10)
    theta = add(a0)
    delta = th - theta
    coef = add(vt + delta * vb)
    length = add(
        t_t + delta * (2.0 * t_b + delta * b_b) - coef * (2.0 * (vt + delta * vb) - coef * n0)
    )
    inv = 1.0 / jnp.sqrt(jnp.maximum(length, 0.0) + eps)
    cross = add(ts + delta * bs - coef * a0) * inv
    d_loc = th_loc - theta
    v1 = [(x + d_loc * y - coef * z) * inv for x, y, z in zip(tt, bb, v0)]

    s1 = apply_h(v1)
    xx = [(x - theta * y - cross * z) * w for x, y, z, w in zip(s0, v0, v1, ip)]
    zz = [x * y for x, y in zip(v1, ip)]
    n1_loc = lanes(inner(v1, v1))
    d1_loc = lanes(inner(v1, s1))
    g_loc = d1_loc / jnp.maximum(n1_loc, 1e-30)
    yy = [(x - cross * y - g_loc * z) * w for x, y, z, w in zip(s1, v0, v1, ip)]
    send_row(2, pack([
        n1_loc, d1_loc, g_loc, inner(v0, v1),
        inner(xx, xx), inner(xx, yy), inner(xx, zz), inner(yy, yy), inner(yy, zz), inner(zz, zz),
        inner(v0, xx), inner(v0, yy), inner(v0, zz), inner(v1, xx), inner(v1, yy), inner(v1, zz),
    ]))
    (n1, d1, g, o01, xx_, xy_, xz_, yy_, yz_, zz_, ax, ay, az, bx, by, bz) = columns(wait_rows(2), 16)
    diag = add(d1)
    gap = (theta - diag) * 0.5
    lowest = (theta + diag) * 0.5 - jnp.sqrt(gap * gap + cross * cross)
    size = jnp.sqrt(cross * cross + (lowest - theta) * (lowest - theta))
    c0 = cross / size
    c1 = (lowest - theta) / size
    e = c1 * (g - diag)
    f0d = c0 * ax + c1 * ay + e * az
    f1d = c0 * bx + c1 * by + e * bz
    f0 = add(f0d)
    f1 = add(f1d)
    square1 = (
        c0 * c0 * xx_ + c1 * c1 * yy_ + e * e * zz_
        + 2.0 * (c0 * c1 * xy_ + c0 * e * xz_ + c1 * e * yz_)
    )
    length1 = add(
        square1 - 2.0 * (f0 * f0d + f1 * f1d) + f0 * f0 * n0 + f1 * f1 * n1 + 2.0 * f0 * f1 * o01
    )
    inv1 = 1.0 / jnp.sqrt(jnp.maximum(length1, 0.0) + eps)
    e_loc = c1 * (g_loc - diag)
    v2 = []
    for q in range(nj):
        new = (c0 * xx[q] + c1 * yy[q] + e_loc * zz[q] - f0 * v0[q] - f1 * v1[q]) * inv1
        nvbuf[q] = new.astype(bf16)
        v2.append(new)

    def out_copy(k, src, dst, which):
        place = lax.rem(t * R + r + k, T * R)
        t2, r2 = place // R, lax.rem(place, R)
        if k == 0:
            return pltpu.make_async_copy(src.at[:, :, half(r2)], dst.at[0, own], out_sem.at[which])
        return pltpu.make_async_remote_copy(
            src.at[:, :, half(r2)], dst.at[0, own], out_send.at[which, k - 1], out_sem.at[which],
            device_id={"sector": s, "term": t2, "rep": r2}, device_id_type=MESH,
        )

    for k in range(T * R):
        out_copy(k, nvbuf, nv_out, 0).start()
    s2 = apply_h(v2)
    for q in range(nj):
        imgbuf[q] = s2[q].astype(bf16)
    for k in range(T * R):
        out_copy(k, imgbuf, img_out, 1).start()
    ritz_out[0] = jnp.sum(lowest)

    for index in range(3):
        some = rows.at[index, pl.ds(0, N - 1)]
        pltpu.make_async_copy(some, some, row_send.at[index]).wait()
    loop(1, R, lambda k: v_copy(k, v_in, vbuf, v_send, vsem).wait_send())
    loop(1, R, lambda k: v_copy(k, p_in, pbuf, p_send, psem).wait_send())
    loop(1, S, lambda k: r_copy(k).wait_send())

    @pl.when(jnp.logical_not(mine))
    def _():
        r_copy(0).wait_send()

    loop(1, T, lambda k: l_copy(k).wait_send())
    for k in range(1, T * R):
        out_copy(k, nvbuf, nv_out, 0).wait_send()
        out_copy(k, imgbuf, img_out, 1).wait_send()
    whole(nv_out, out_sem.at[0])
    whole(img_out, out_sem.at[1])


def solution(mesh):
    S, T, R = mesh.shape["sector"], mesh.shape["term"], mesh.shape["rep"]

    def local(start_vector, precond, left_env, right_env, blocks_used):
        SB, B, H = start_vector.shape[1:]
        nj = SB // (T * R)
        N = S * T * R
        count = float(start_vector.size * S * R)
        dma = pltpu.SemaphoreType.DMA
        hbm = pl.BlockSpec(memory_space=pltpu.HBM)
        vmem = pl.BlockSpec(memory_space=pltpu.VMEM)
        smem = pl.BlockSpec(memory_space=pltpu.SMEM)
        shape = jax.ShapeDtypeStruct(start_vector.shape, bf16)
        vector, image, ritz = pl.pallas_call(
            functools.partial(kernel, S, T, R, nj, count),
            out_shape=(shape, shape, jax.ShapeDtypeStruct((1,), f32)),
            in_specs=[hbm, hbm, hbm, hbm, smem],
            out_specs=(vmem, vmem, smem),
            scratch_shapes=[
                pltpu.VMEM((R * nj, B, H), bf16),
                pltpu.VMEM((nj, B, B), bf16),
                pltpu.VMEM((nj, B, B), bf16),
                pltpu.VMEM((T, nj, B, B), bf16),
                pltpu.VMEM((T, nj, B, B), bf16),
                pltpu.VMEM((nj, B, B), bf16),
                pltpu.VMEM((nj, B, B), bf16),
                pltpu.VMEM((3, N, 1, 128), f32),
                dma, dma, dma, dma, dma, dma((3,)), dma((3,)), dma((R,)), dma((R,)), dma((T,)),
                dma((S,)), dma((2,)), dma((2, T * R)),
            ],
            compiler_params=pltpu.CompilerParams(
                collective_id=0, has_side_effects=True, vmem_limit_bytes=60 * 2**20
            ),
            name="davidson",
        )(start_vector, precond, left_env, right_env, blocks_used)
        return vector.astype(f32), image.astype(f32), ritz

    in_specs = (
        P(("groups", "sector"), None, None, "rep"),
        P(("groups", "sector"), None, None, "rep"),
        P("term", ("groups", "sector"), None, None, None),
        P("term", "sector", "groups", None, "rep"),
        P("term", ("groups", "sector"), None),
    )
    out_specs = (
        P(("groups", "sector"), None, None, "rep"),
        P(("groups", "sector"), None, None, "rep"),
        P("groups"),
    )
    return jax.shard_map(local, mesh=mesh, in_specs=in_specs, out_specs=out_specs, check_vma=False)
```

```python
import functools
import jax
import jax.numpy as jnp
from jax import lax
from jax.experimental import pallas as pl
from jax.experimental.pallas import tpu as pltpu
from jax.sharding import PartitionSpec as P

eps = 1e-06
MESH = pl.DeviceIdType.MESH
f32 = jnp.float32
bf16 = jnp.bfloat16


def loop(low, high, body):
    if high - low <= 16:
        for k in range(low, high):
            body(k)
    else:
        lax.fori_loop(low, high, lambda k, c: (body(k), c)[1], 0)


def pack(sums):
    lane = lax.broadcasted_iota(jnp.int32, (1, 128), 1)
    row = jnp.zeros((1, 128), f32)
    for k, value in enumerate(sums):
        if value.shape != (1, 1):
            value = jnp.sum(value, axis=1, keepdims=True)
        row = row + jnp.where(lane == k, value, 0.0)
    return row


def partial(products):
    total = products[0]
    for other in products[1:]:
        total = total + other
    return jnp.sum(total, axis=0, keepdims=True)


def kernel(
    S, T, R, nj, count,
    v_in, p_in, l_in, r_in, used,
    nv_out, img_out, ritz_out,
    vloc, vbuf, pbuf, lbuf, rbuf, nvbuf, imgbuf, rows,
    local_sem, vsem, psem, lsem, rsem, row_sem, row_send, v_send, p_send, l_send, r_send,
    out_sem, out_send,
):
    N = S * T * R
    SB = nj * T * R
    B = lbuf.shape[-1]
    H = B // R
    s, t, r = lax.axis_index("sector"), lax.axis_index("term"), lax.axis_index("rep")
    me = (s * T + t) * R + r

    def device(rank):
        return {"sector": rank // (T * R), "term": lax.rem(rank // R, T), "rep": lax.rem(rank, R)}

    order = [a for a in (S - 1, 1) if 0 < a] if S > 1 else []
    order = list(dict.fromkeys(order + list(range(2, S - 1)))) + [0]
    peers = [(a, b, c) for a in order for b in reversed(range(T)) for c in reversed(range(R))][:-1]

    def each_peer(body):
        if N <= 16:
            for a, b, c in peers:
                body({"sector": lax.rem(s + a, S), "term": lax.rem(t + b, T), "rep": lax.rem(r + c, R)})
        else:
            lax.fori_loop(1, N, lambda k, c: (body(device(lax.rem(me + k, N))), c)[1], 0)

    def first(t2, r2):
        return (t2 * R + r2) * nj

    def half(r2):
        return pl.ds(pl.multiple_of(r2 * H, H), H)

    C = B // 2
    tiles = ((pl.ds(C, C), pl.ds(0, B)), (pl.ds(0, C), pl.ds(0, C)))

    own = pl.ds(first(t, r), nj)
    load = pltpu.make_async_copy(v_in.at[0, pl.ds(t * R * nj, R * nj)], vloc, local_sem)
    load.start()
    pltpu.make_async_copy(v_in.at[0, own], vbuf.at[:, :, half(r)], vsem).start()
    pltpu.make_async_copy(p_in.at[0, own], pbuf.at[:, :, half(r)], psem).start()
    for rows_of, lanes_of in tiles:
        pltpu.make_async_copy(
            l_in.at[0, 0, own, rows_of, lanes_of], lbuf.at[t, :, rows_of, lanes_of], lsem
        ).start()

    barrier = pltpu.get_barrier_semaphore()

    def greet(peer):
        pl.semaphore_signal(barrier, inc=1, device_id=peer, device_id_type=MESH)

    each_peer(greet)

    load.wait()
    lane = lax.broadcasted_iota(jnp.int32, (1, 128), 1)
    local_v = [vloc[k].astype(f32) for k in range(R * nj)]
    row = pack([partial([x * x for x in local_v])])
    for j in range(SB):
        row = row + jnp.where(lane == 8 + j, used[0, 0, j].astype(f32), 0.0)

    def send_row(index, row):
        rows[index, me] = row

        def one(peer):
            pltpu.make_async_remote_copy(
                rows.at[index, me], rows.at[index, me], row_send.at[index], row_sem.at[index],
                device_id=peer, device_id_type=MESH,
            ).start()

        each_peer(one)

    def wait_rows(index):
        some = rows.at[index, pl.ds(0, N - 1)]
        pltpu.make_async_copy(some, some, row_sem.at[index]).wait()
        return rows[index].reshape(N, 128)

    pl.semaphore_wait(barrier, N - 1)
    send_row(0, row)

    def v_copy(k, src, dst, sem, recv):
        r2 = lax.rem(r + k, R)
        return pltpu.make_async_remote_copy(
            src.at[0, pl.ds(first(t, r2), nj)], dst.at[:, :, half(r)], sem.at[k - 1], recv,
            device_id={"sector": s, "term": t, "rep": r2}, device_id_type=MESH,
        )

    def l_copy(k, which):
        t2 = lax.rem(t + k, T)
        rows_of, lanes_of = tiles[which]
        return pltpu.make_async_remote_copy(
            l_in.at[0, 0, pl.ds(first(t2, r), nj), rows_of, lanes_of],
            lbuf.at[t, :, rows_of, lanes_of], l_send.at[k - 1, which], lsem,
            device_id={"sector": s, "term": t2, "rep": r}, device_id_type=MESH,
        )

    owner = s // nj
    owner_t, owner_r, slot = owner // R, lax.rem(owner, R), lax.rem(s, nj)
    mine = jnp.logical_and(owner_t == t, owner_r == r)

    def r_copy(k, rows_of):
        i2 = lax.rem(s + k, S)
        return pltpu.make_async_remote_copy(
            r_in.at[0, 0, i2, rows_of], rbuf.at[t, slot, rows_of, half(r)], r_send.at[k], rsem,
            device_id={"sector": i2, "term": owner_t, "rep": owner_r}, device_id_type=MESH,
        )

    loop(1, R, lambda k: v_copy(k, v_in, vbuf, v_send, vsem).start())
    loop(1, R, lambda k: v_copy(k, p_in, pbuf, p_send, psem).start())
    def right(rows_of, finish):
        for k in order[:-1]:
            copy = r_copy(k, rows_of)
            copy.wait_send() if finish else copy.start()

        if not finish:

            @pl.when(mine)
            def _():
                pltpu.make_async_copy(
                    r_in.at[0, 0, s, rows_of], rbuf.at[t, slot, rows_of, half(r)], rsem
                ).start()

        @pl.when(jnp.logical_not(mine))
        def _():
            copy = r_copy(0, rows_of)
            copy.wait_send() if finish else copy.start()

    def both_halves(finish):
        pl.when(r == 0)(lambda: right(pl.ds(0, B), finish))
        pl.when(r != 0)(lambda: right(pl.ds(C, C), finish))

    both_halves(False)

    loop(1, T, lambda k: l_copy(k, 0).start())
    loop(1, T, lambda k: l_copy(k, 1).start())

    def whole(ref, sem):
        pltpu.make_async_copy(ref, ref, sem).wait()

    m0 = wait_rows(0)
    square = jnp.sum(m0[:, 0:1], axis=0, keepdims=True) / count
    scale = 1.0 / jnp.sqrt(square + eps)
    masks = []
    for t2 in range(T):
        peer_row = rows[0, (s * T + t2) * R + r]
        masks.append([
            jnp.sum(jnp.where(lane == 8 + first(t, r) + q, peer_row, 0.0), axis=1, keepdims=True)
            for q in range(nj)
        ])
    whole(vbuf, vsem)
    v0 = [vbuf[q].astype(f32) * scale for q in range(nj)]
    whole(pbuf, psem)
    ip = [1.0 / pbuf[q].astype(f32) for q in range(nj)]
    whole(lbuf.at[:, :, pl.ds(0, 3 * B // 4)], lsem)
    whole(rbuf.at[:, :, pl.ds(0, 3 * B // 4)], rsem)
    for buf in (lbuf, rbuf):
        for t2 in range(T):
            for q in range(nj):
                buf[t2, q, 0:C, C:B] = buf[t2, q, C:B, 0:C].T

    def apply_h(v):
        result = []
        for q in range(nj):
            rounded = v[q].astype(bf16)
            total = None
            for t2 in range(T):
                mixed = jnp.dot(lbuf[t2, q], rounded, preferred_element_type=f32)
                mixed = (mixed * masks[t2][q]).astype(bf16)
                piece = lax.dot_general(
                    mixed, rbuf[t2, q], (((1,), (1,)), ((), ())), preferred_element_type=f32
                )
                total = piece if total is None else total + piece
            result.append(total)
        return result

    def inner(x, y):
        return partial([a * b for a, b in zip(x, y)])

    def lanes(x):
        return jnp.sum(x, axis=1, keepdims=True)

    def columns(m, n):
        return [m[:, k:k + 1] for k in range(n)]

    def add(x):
        return jnp.sum(x, axis=0, keepdims=True) / count

    s0 = apply_h(v0)
    n_loc = lanes(inner(v0, v0))
    a_loc = lanes(inner(v0, s0))
    th_loc = a_loc / jnp.maximum(n_loc, 1e-30)
    bb = [a * b for a, b in zip(v0, ip)]
    tt = [(a - th_loc * b) * c for a, b, c in zip(s0, v0, ip)]
    send_row(1, pack([
        n_loc, a_loc, th_loc, inner(v0, tt), inner(v0, bb), inner(tt, tt), inner(tt, bb),
        inner(bb, bb), inner(tt, s0), inner(bb, s0),
    ]))
    n0, a0, th, vt, vb, t_t, t_b, b_b, ts, bs = columns(wait_rows(1), 10)
    theta = add(a0)
    delta = th - theta
    coef = add(vt + delta * vb)
    length = add(
        t_t + delta * (2.0 * t_b + delta * b_b) - coef * (2.0 * (vt + delta * vb) - coef * n0)
    )
    inv = 1.0 / jnp.sqrt(jnp.maximum(length, 0.0) + eps)
    cross = add(ts + delta * bs - coef * a0) * inv
    d_loc = th_loc - theta
    v1 = [(x + d_loc * y - coef * z) * inv for x, y, z in zip(tt, bb, v0)]

    s1 = apply_h(v1)
    xx = [(x - theta * y - cross * z) * w for x, y, z, w in zip(s0, v0, v1, ip)]
    zz = [x * y for x, y in zip(v1, ip)]
    n1_loc = lanes(inner(v1, v1))
    d1_loc = lanes(inner(v1, s1))
    g_loc = d1_loc / jnp.maximum(n1_loc, 1e-30)
    yy = [(x - cross * y - g_loc * z) * w for x, y, z, w in zip(s1, v0, v1, ip)]
    send_row(2, pack([
        n1_loc, d1_loc, g_loc, inner(v0, v1),
        inner(xx, xx), inner(xx, yy), inner(xx, zz), inner(yy, yy), inner(yy, zz), inner(zz, zz),
        inner(v0, xx), inner(v0, yy), inner(v0, zz), inner(v1, xx), inner(v1, yy), inner(v1, zz),
    ]))
    (n1, d1, g, o01, xx_, xy_, xz_, yy_, yz_, zz_, ax, ay, az, bx, by, bz) = columns(wait_rows(2), 16)
    diag = add(d1)
    gap = (theta - diag) * 0.5
    lowest = (theta + diag) * 0.5 - jnp.sqrt(gap * gap + cross * cross)
    size = jnp.sqrt(cross * cross + (lowest - theta) * (lowest - theta))
    c0 = cross / size
    c1 = (lowest - theta) / size
    e = c1 * (g - diag)
    f0d = c0 * ax + c1 * ay + e * az
    f1d = c0 * bx + c1 * by + e * bz
    f0 = add(f0d)
    f1 = add(f1d)
    square1 = (
        c0 * c0 * xx_ + c1 * c1 * yy_ + e * e * zz_
        + 2.0 * (c0 * c1 * xy_ + c0 * e * xz_ + c1 * e * yz_)
    )
    length1 = add(
        square1 - 2.0 * (f0 * f0d + f1 * f1d) + f0 * f0 * n0 + f1 * f1 * n1 + 2.0 * f0 * f1 * o01
    )
    inv1 = 1.0 / jnp.sqrt(jnp.maximum(length1, 0.0) + eps)
    e_loc = c1 * (g_loc - diag)
    v2 = []
    for q in range(nj):
        new = (c0 * xx[q] + c1 * yy[q] + e_loc * zz[q] - f0 * v0[q] - f1 * v1[q]) * inv1
        nvbuf[q] = new.astype(bf16)
        v2.append(new)

    def out_copy(k, src, dst, which):
        place = lax.rem(t * R + r + k, T * R)
        t2, r2 = place // R, lax.rem(place, R)
        if k == 0:
            return pltpu.make_async_copy(src.at[:, :, half(r2)], dst.at[0, own], out_sem.at[which])
        return pltpu.make_async_remote_copy(
            src.at[:, :, half(r2)], dst.at[0, own], out_send.at[which, k - 1], out_sem.at[which],
            device_id={"sector": s, "term": t2, "rep": r2}, device_id_type=MESH,
        )

    for k in range(T * R):
        out_copy(k, nvbuf, nv_out, 0).start()
    s2 = apply_h(v2)
    for q in range(nj):
        imgbuf[q] = s2[q].astype(bf16)
    for k in range(T * R):
        out_copy(k, imgbuf, img_out, 1).start()
    ritz_out[0] = jnp.sum(lowest)

    for index in range(3):
        some = rows.at[index, pl.ds(0, N - 1)]
        pltpu.make_async_copy(some, some, row_send.at[index]).wait()
    loop(1, R, lambda k: v_copy(k, v_in, vbuf, v_send, vsem).wait_send())
    loop(1, R, lambda k: v_copy(k, p_in, pbuf, p_send, psem).wait_send())
    both_halves(True)
    loop(1, T, lambda k: l_copy(k, 0).wait_send())
    loop(1, T, lambda k: l_copy(k, 1).wait_send())
    for k in range(1, T * R):
        out_copy(k, nvbuf, nv_out, 0).wait_send()
        out_copy(k, imgbuf, img_out, 1).wait_send()
    whole(nv_out, out_sem.at[0])
    whole(img_out, out_sem.at[1])


def widen(a_in, b_in, a_out, b_out, a_buf, b_buf, a_wide, b_wide, load_sem, store_sem):
    sets = ((a_in, a_buf, a_wide, a_out), (b_in, b_buf, b_wide, b_out))
    places = [(w, j) for j in range(a_buf.shape[0]) for w in range(2)]

    def load(w, j):
        return pltpu.make_async_copy(sets[w][0].at[0, j], sets[w][1].at[j], load_sem.at[w, j])

    def store(w, j):
        return pltpu.make_async_copy(sets[w][2].at[j], sets[w][3].at[0, j], store_sem.at[w, j])

    for place in places:
        load(*place).start()
    for w, j in places:
        load(w, j).wait()
        sets[w][2][j] = sets[w][1][j].astype(f32)
        store(w, j).start()
    for place in places:
        store(*place).wait()


def solution(mesh):
    S, T, R = mesh.shape["sector"], mesh.shape["term"], mesh.shape["rep"]

    def local(start_vector, precond, left_env, right_env, blocks_used):
        SB, B, H = start_vector.shape[1:]
        nj = SB // (T * R)
        N = S * T * R
        count = float(start_vector.size * S * R)
        dma = pltpu.SemaphoreType.DMA
        hbm = pl.BlockSpec(memory_space=pltpu.HBM)
        vmem = pl.BlockSpec(memory_space=pltpu.VMEM)
        smem = pl.BlockSpec(memory_space=pltpu.SMEM)
        shape = jax.ShapeDtypeStruct(start_vector.shape, bf16)
        vector, image, ritz = pl.pallas_call(
            functools.partial(kernel, S, T, R, nj, count),
            out_shape=(shape, shape, jax.ShapeDtypeStruct((1,), f32)),
            in_specs=[hbm, hbm, hbm, hbm, smem],
            out_specs=(vmem, vmem, smem),
            scratch_shapes=[
                pltpu.VMEM((R * nj, B, H), bf16),
                pltpu.VMEM((nj, B, B), bf16),
                pltpu.VMEM((nj, B, B), bf16),
                pltpu.VMEM((T, nj, B, B), bf16),
                pltpu.VMEM((T, nj, B, B), bf16),
                pltpu.VMEM((nj, B, B), bf16),
                pltpu.VMEM((nj, B, B), bf16),
                pltpu.VMEM((3, N, 1, 128), f32),
                dma, dma, dma, dma, dma, dma((3,)), dma((3,)), dma((R,)), dma((R,)), dma((T, 2)),
                dma((S,)), dma((2,)), dma((2, T * R)),
            ],
            compiler_params=pltpu.CompilerParams(
                collective_id=0, has_side_effects=True, vmem_limit_bytes=60 * 2**20
            ),
            name="davidson",
        )(start_vector, precond, left_env, right_env, blocks_used)
        wide = jax.ShapeDtypeStruct(start_vector.shape, f32)
        vector, image = pl.pallas_call(
            widen,
            out_shape=(wide, wide),
            in_specs=[hbm, hbm],
            out_specs=(hbm, hbm),
            scratch_shapes=[
                pltpu.VMEM((SB, B, H), bf16), pltpu.VMEM((SB, B, H), bf16),
                pltpu.VMEM((SB, B, H), f32), pltpu.VMEM((SB, B, H), f32),
                dma((2, SB)), dma((2, SB)),
            ],
            compiler_params=pltpu.CompilerParams(vmem_limit_bytes=60 * 2**20),
            name="widen",
        )(vector, image)
        return vector, image, ritz

    in_specs = (
        P(("groups", "sector"), None, None, "rep"),
        P(("groups", "sector"), None, None, "rep"),
        P("term", ("groups", "sector"), None, None, None),
        P("term", "sector", "groups", None, "rep"),
        P("term", ("groups", "sector"), None),
    )
    out_specs = (
        P(("groups", "sector"), None, None, "rep"),
        P(("groups", "sector"), None, None, "rep"),
        P("groups"),
    )
    return jax.shard_map(local, mesh=mesh, in_specs=in_specs, out_specs=out_specs, check_vma=False)
```

```python
import functools
import jax
import jax.numpy as jnp
from jax import lax
from jax.experimental import pallas as pl
from jax.experimental.pallas import tpu as pltpu
from jax.sharding import PartitionSpec as P

eps = 1e-06
MESH = pl.DeviceIdType.MESH
f32 = jnp.float32
bf16 = jnp.bfloat16


def loop(low, high, body):
    if high - low <= 16:
        for k in range(low, high):
            body(k)
    else:
        lax.fori_loop(low, high, lambda k, c: (body(k), c)[1], 0)


def pack(sums):
    lane = lax.broadcasted_iota(jnp.int32, (1, 128), 1)
    row = jnp.zeros((1, 128), f32)
    for k, value in enumerate(sums):
        if value.shape != (1, 1):
            value = jnp.sum(value, axis=1, keepdims=True)
        row = row + jnp.where(lane == k, value, 0.0)
    return row


def partial(products):
    total = products[0]
    for other in products[1:]:
        total = total + other
    return jnp.sum(total, axis=0, keepdims=True)


def kernel(
    S, T, R, nj, count,
    v_in, p_in, l_in, r_in, used,
    nv_out, img_out, ritz_out,
    vloc, ploc, vbuf, pbuf, lbuf, rbuf, s0buf, s1buf, imgbuf, s0in, s1in, nvbuf, rows,
    local_sem, vsem, psem, lsem, rsem, row_sem, row_send, v_send, p_send, l_send, r_send,
    out_sem, out_send, ploc_sem, nv_sem,
):
    N = S * T * R
    SB = nj * T * R
    B = lbuf.shape[-1]
    H = B // R
    s, t, r = lax.axis_index("sector"), lax.axis_index("term"), lax.axis_index("rep")
    me = (s * T + t) * R + r

    def device(rank):
        return {"sector": rank // (T * R), "term": lax.rem(rank // R, T), "rep": lax.rem(rank, R)}

    order = [a for a in (S - 1, 1) if 0 < a] if S > 1 else []
    order = list(dict.fromkeys(order + list(range(2, S - 1)))) + [0]
    peers = [(a, b, c) for a in order for b in reversed(range(T)) for c in reversed(range(R))][:-1]

    def each_peer(body):
        if N <= 16:
            for a, b, c in peers:
                body({"sector": lax.rem(s + a, S), "term": lax.rem(t + b, T), "rep": lax.rem(r + c, R)})
        else:
            lax.fori_loop(1, N, lambda k, c: (body(device(lax.rem(me + k, N))), c)[1], 0)

    def first(t2, r2):
        return (t2 * R + r2) * nj

    def half(r2):
        return pl.ds(pl.multiple_of(r2 * H, H), H)

    C = B // 2
    tiles = ((pl.ds(C, C), pl.ds(0, B)), (pl.ds(0, C), pl.ds(0, C)))

    own = pl.ds(first(t, r), nj)
    load = pltpu.make_async_copy(v_in.at[0], vloc, local_sem)
    load.start()
    pltpu.make_async_copy(v_in.at[0, own], vbuf.at[:, :, half(r)], vsem).start()
    pltpu.make_async_copy(p_in.at[0, own], pbuf.at[:, :, half(r)], psem).start()
    for rows_of, lanes_of in tiles:
        pltpu.make_async_copy(
            l_in.at[0, 0, own, rows_of, lanes_of], lbuf.at[t, :, rows_of, lanes_of], lsem
        ).start()

    barrier = pltpu.get_barrier_semaphore()

    def greet(peer):
        pl.semaphore_signal(barrier, inc=1, device_id=peer, device_id_type=MESH)

    each_peer(greet)

    load.wait()
    lane = lax.broadcasted_iota(jnp.int32, (1, 128), 1)
    local_v = [vloc[t * R * nj + k].astype(f32) for k in range(R * nj)]
    row = pack([partial([x * x for x in local_v])])
    for j in range(SB):
        row = row + jnp.where(lane == 8 + j, used[0, 0, j].astype(f32), 0.0)

    def send_row(index, row):
        rows[index, me] = row

        def one(peer):
            pltpu.make_async_remote_copy(
                rows.at[index, me], rows.at[index, me], row_send.at[index], row_sem.at[index],
                device_id=peer, device_id_type=MESH,
            ).start()

        each_peer(one)

    def wait_rows(index):
        some = rows.at[index, pl.ds(0, N - 1)]
        pltpu.make_async_copy(some, some, row_sem.at[index]).wait()
        return rows[index].reshape(N, 128)

    pl.semaphore_wait(barrier, N - 1)
    send_row(0, row)

    p_load = pltpu.make_async_copy(p_in.at[0], ploc, ploc_sem)
    p_load.start()

    def v_copy(k, src, dst, sem, recv):
        r2 = lax.rem(r + k, R)
        return pltpu.make_async_remote_copy(
            src.at[0, pl.ds(first(t, r2), nj)], dst.at[:, :, half(r)], sem.at[k - 1], recv,
            device_id={"sector": s, "term": t, "rep": r2}, device_id_type=MESH,
        )

    def l_copy(k, which):
        t2 = lax.rem(t + k, T)
        rows_of, lanes_of = tiles[which]
        return pltpu.make_async_remote_copy(
            l_in.at[0, 0, pl.ds(first(t2, r), nj), rows_of, lanes_of],
            lbuf.at[t, :, rows_of, lanes_of], l_send.at[k - 1, which], lsem,
            device_id={"sector": s, "term": t2, "rep": r}, device_id_type=MESH,
        )

    owner = s // nj
    owner_t, owner_r, slot = owner // R, lax.rem(owner, R), lax.rem(s, nj)
    mine = jnp.logical_and(owner_t == t, owner_r == r)

    def r_copy(k, rows_of):
        i2 = lax.rem(s + k, S)
        return pltpu.make_async_remote_copy(
            r_in.at[0, 0, i2, rows_of], rbuf.at[t, slot, rows_of, half(r)], r_send.at[k], rsem,
            device_id={"sector": i2, "term": owner_t, "rep": owner_r}, device_id_type=MESH,
        )

    loop(1, R, lambda k: v_copy(k, v_in, vbuf, v_send, vsem).start())
    loop(1, R, lambda k: v_copy(k, p_in, pbuf, p_send, psem).start())
    def right(rows_of, finish):
        for k in order[:-1]:
            copy = r_copy(k, rows_of)
            copy.wait_send() if finish else copy.start()

        if not finish:

            @pl.when(mine)
            def _():
                pltpu.make_async_copy(
                    r_in.at[0, 0, s, rows_of], rbuf.at[t, slot, rows_of, half(r)], rsem
                ).start()

        @pl.when(jnp.logical_not(mine))
        def _():
            copy = r_copy(0, rows_of)
            copy.wait_send() if finish else copy.start()

    def both_halves(finish):
        pl.when(r == 0)(lambda: right(pl.ds(0, B), finish))
        pl.when(r != 0)(lambda: right(pl.ds(C, C), finish))

    both_halves(False)

    loop(1, T, lambda k: l_copy(k, 0).start())
    loop(1, T, lambda k: l_copy(k, 1).start())

    def whole(ref, sem):
        pltpu.make_async_copy(ref, ref, sem).wait()

    m0 = wait_rows(0)
    square = jnp.sum(m0[:, 0:1], axis=0, keepdims=True) / count
    scale = 1.0 / jnp.sqrt(square + eps)
    masks = []
    for t2 in range(T):
        peer_row = rows[0, (s * T + t2) * R + r]
        masks.append([
            jnp.sum(jnp.where(lane == 8 + first(t, r) + q, peer_row, 0.0), axis=1, keepdims=True)
            for q in range(nj)
        ])
    whole(vbuf, vsem)
    v0 = [vbuf[q].astype(f32) * scale for q in range(nj)]
    whole(pbuf, psem)
    ip = [1.0 / pbuf[q].astype(f32) for q in range(nj)]
    whole(lbuf.at[:, :, pl.ds(0, 3 * B // 4)], lsem)
    whole(rbuf.at[:, :, pl.ds(0, 3 * B // 4)], rsem)
    for buf in (lbuf, rbuf):
        for t2 in range(T):
            for q in range(nj):
                buf[t2, q, 0:C, C:B] = buf[t2, q, C:B, 0:C].T

    def apply_h(v):
        result = []
        for q in range(nj):
            rounded = v[q].astype(bf16)
            total = None
            for t2 in range(T):
                mixed = jnp.dot(lbuf[t2, q], rounded, preferred_element_type=f32)
                mixed = (mixed * masks[t2][q]).astype(bf16)
                piece = lax.dot_general(
                    mixed, rbuf[t2, q], (((1,), (1,)), ((), ())), preferred_element_type=f32
                )
                total = piece if total is None else total + piece
            result.append(total)
        return result

    def inner(x, y):
        return partial([a * b for a, b in zip(x, y)])

    def lanes(x):
        return jnp.sum(x, axis=1, keepdims=True)

    def columns(m, n):
        return [m[:, k:k + 1] for k in range(n)]

    def add(x):
        return jnp.sum(x, axis=0, keepdims=True) / count

    def out_copy(k, src, dst, which):
        place = lax.rem(t * R + r + k, T * R)
        t2, r2 = place // R, lax.rem(place, R)
        if k == 0:
            return pltpu.make_async_copy(src.at[:, :, half(r2)], dst.at[own], out_sem.at[which])
        return pltpu.make_async_remote_copy(
            src.at[:, :, half(r2)], dst.at[own], out_send.at[which, k - 1], out_sem.at[which],
            device_id={"sector": s, "term": t2, "rep": r2}, device_id_type=MESH,
        )

    sent = ((s0buf, s0in), (s1buf, s1in), (imgbuf, img_out.at[0]))

    def spread(which, value):
        src, dst = sent[which]
        for q in range(nj):
            src[q] = value[q].astype(src.dtype)
        for k in range(T * R):
            out_copy((k + 1) % (T * R), src, dst, which).start()

    s0 = apply_h(v0)
    n_loc = lanes(inner(v0, v0))
    a_loc = lanes(inner(v0, s0))
    th_loc = a_loc / jnp.maximum(n_loc, 1e-30)
    bb = [a * b for a, b in zip(v0, ip)]
    tt = [(a - th_loc * b) * c for a, b, c in zip(s0, v0, ip)]
    send_row(1, pack([
        n_loc, a_loc, th_loc, inner(v0, tt), inner(v0, bb), inner(tt, tt), inner(tt, bb),
        inner(bb, bb), inner(tt, s0), inner(bb, s0),
    ]))
    spread(0, s0)
    n0, a0, th, vt, vb, t_t, t_b, b_b, ts, bs = columns(wait_rows(1), 10)
    theta = add(a0)
    delta = th - theta
    coef = add(vt + delta * vb)
    length = add(
        t_t + delta * (2.0 * t_b + delta * b_b) - coef * (2.0 * (vt + delta * vb) - coef * n0)
    )
    inv = 1.0 / jnp.sqrt(jnp.maximum(length, 0.0) + eps)
    cross = add(ts + delta * bs - coef * a0) * inv
    d_loc = th_loc - theta
    v1 = [(x + d_loc * y - coef * z) * inv for x, y, z in zip(tt, bb, v0)]

    s1 = apply_h(v1)
    xx = [(x - theta * y - cross * z) * w for x, y, z, w in zip(s0, v0, v1, ip)]
    zz = [x * y for x, y in zip(v1, ip)]
    n1_loc = lanes(inner(v1, v1))
    d1_loc = lanes(inner(v1, s1))
    g_loc = d1_loc / jnp.maximum(n1_loc, 1e-30)
    yy = [(x - cross * y - g_loc * z) * w for x, y, z, w in zip(s1, v0, v1, ip)]
    send_row(2, pack([
        n1_loc, d1_loc, g_loc, inner(v0, v1),
        inner(xx, xx), inner(xx, yy), inner(xx, zz), inner(yy, yy), inner(yy, zz), inner(zz, zz),
        inner(v0, xx), inner(v0, yy), inner(v0, zz), inner(v1, xx), inner(v1, yy), inner(v1, zz),
    ]))
    spread(1, s1)
    (n1, d1, g, o01, xx_, xy_, xz_, yy_, yz_, zz_, ax, ay, az, bx, by, bz) = columns(wait_rows(2), 16)
    diag = add(d1)
    gap = (theta - diag) * 0.5
    lowest = (theta + diag) * 0.5 - jnp.sqrt(gap * gap + cross * cross)
    size = jnp.sqrt(cross * cross + (lowest - theta) * (lowest - theta))
    c0 = cross / size
    c1 = (lowest - theta) / size
    e = c1 * (g - diag)
    f0d = c0 * ax + c1 * ay + e * az
    f1d = c0 * bx + c1 * by + e * bz
    f0 = add(f0d)
    f1 = add(f1d)
    square1 = (
        c0 * c0 * xx_ + c1 * c1 * yy_ + e * e * zz_
        + 2.0 * (c0 * c1 * xy_ + c0 * e * xz_ + c1 * e * yz_)
    )
    length1 = add(
        square1 - 2.0 * (f0 * f0d + f1 * f1d) + f0 * f0 * n0 + f1 * f1 * n1 + 2.0 * f0 * f1 * o01
    )
    inv1 = 1.0 / jnp.sqrt(jnp.maximum(length1, 0.0) + eps)
    e_loc = c1 * (g_loc - diag)
    v2 = []
    for q in range(nj):
        new = (c0 * xx[q] + c1 * yy[q] + e_loc * zz[q] - f0 * v0[q] - f1 * v1[q]) * inv1
        v2.append(new)

    s2 = apply_h(v2)
    spread(2, s2)

    p_load.wait()
    whole(s0in, out_sem.at[0])
    whole(s1in, out_sem.at[1])
    for j in range(SB):
        v0_j = vloc[j].astype(f32) * scale
        ip_j = 1.0 / ploc[j].astype(f32)
        s0_j, s1_j = s0in[j], s1in[j].astype(f32)
        r0_j = s0_j - theta * v0_j
        v1_j = (r0_j * ip_j - coef * v0_j) * inv
        r1_j = c0 * (r0_j - cross * v1_j) + c1 * (s1_j - cross * v0_j - diag * v1_j)
        nvbuf[j] = (r1_j * ip_j - f0 * v0_j - f1 * v1_j) * inv1
    nv_store = pltpu.make_async_copy(nvbuf, nv_out.at[0], nv_sem)
    nv_store.start()
    ritz_out[0] = jnp.sum(lowest)

    for index in range(3):
        some = rows.at[index, pl.ds(0, N - 1)]
        pltpu.make_async_copy(some, some, row_send.at[index]).wait()
    loop(1, R, lambda k: v_copy(k, v_in, vbuf, v_send, vsem).wait_send())
    loop(1, R, lambda k: v_copy(k, p_in, pbuf, p_send, psem).wait_send())
    both_halves(True)
    loop(1, T, lambda k: l_copy(k, 0).wait_send())
    loop(1, T, lambda k: l_copy(k, 1).wait_send())
    for which, (src, dst) in enumerate(sent):
        for k in range(1, T * R):
            out_copy(k, src, dst, which).wait_send()
    whole(img_out.at[0], out_sem.at[2])
    nv_store.wait()


def widen(a_in, b_in, a_out, b_out, a_buf, b_buf, b_wide, load_sem, store_sem):
    sets = ((a_in, a_buf, a_buf, a_out), (b_in, b_buf, b_wide, b_out))
    places = [(w, j) for j in range(a_buf.shape[0]) for w in range(2)]

    def load(w, j):
        return pltpu.make_async_copy(sets[w][0].at[0, j], sets[w][1].at[j], load_sem.at[w, j])

    def store(w, j):
        return pltpu.make_async_copy(sets[w][2].at[j], sets[w][3].at[0, j], store_sem.at[w, j])

    for place in places:
        load(*place).start()
    for w, j in places:
        load(w, j).wait()
        if w == 1:
            b_wide[j] = b_buf[j].astype(f32)
        store(w, j).start()
    for place in places:
        store(*place).wait()


def solution(mesh):
    S, T, R = mesh.shape["sector"], mesh.shape["term"], mesh.shape["rep"]

    def local(start_vector, precond, left_env, right_env, blocks_used):
        SB, B, H = start_vector.shape[1:]
        nj = SB // (T * R)
        N = S * T * R
        count = float(start_vector.size * S * R)
        dma = pltpu.SemaphoreType.DMA
        hbm = pl.BlockSpec(memory_space=pltpu.HBM)
        smem = pl.BlockSpec(memory_space=pltpu.SMEM)
        shape = jax.ShapeDtypeStruct(start_vector.shape, bf16)
        wide = jax.ShapeDtypeStruct(start_vector.shape, f32)
        vector, image, ritz = pl.pallas_call(
            functools.partial(kernel, S, T, R, nj, count),
            out_shape=(wide, shape, jax.ShapeDtypeStruct((1,), f32)),
            in_specs=[hbm, hbm, hbm, hbm, smem],
            out_specs=(hbm, hbm, smem),
            scratch_shapes=[
                pltpu.VMEM((SB, B, H), bf16),
                pltpu.VMEM((SB, B, H), bf16),
                pltpu.VMEM((nj, B, B), bf16),
                pltpu.VMEM((nj, B, B), bf16),
                pltpu.VMEM((T, nj, B, B), bf16),
                pltpu.VMEM((T, nj, B, B), bf16),
                pltpu.VMEM((nj, B, B), f32),
                pltpu.VMEM((nj, B, B), bf16),
                pltpu.VMEM((nj, B, B), bf16),
                pltpu.VMEM((SB, B, H), f32),
                pltpu.VMEM((SB, B, H), bf16),
                pltpu.VMEM((SB, B, H), f32),
                pltpu.VMEM((3, N, 1, 128), f32),
                dma, dma, dma, dma, dma, dma((3,)), dma((3,)), dma((R,)), dma((R,)), dma((T, 2)),
                dma((S,)), dma((3,)), dma((3, T * R)), dma, dma,
            ],
            compiler_params=pltpu.CompilerParams(
                collective_id=0, has_side_effects=True, vmem_limit_bytes=60 * 2**20
            ),
            name="davidson",
        )(start_vector, precond, left_env, right_env, blocks_used)
        vector, image = pl.pallas_call(
            widen,
            out_shape=(wide, wide),
            in_specs=[hbm, hbm],
            out_specs=(hbm, hbm),
            scratch_shapes=[
                pltpu.VMEM((SB, B, H), f32), pltpu.VMEM((SB, B, H), bf16),
                pltpu.VMEM((SB, B, H), f32),
                dma((2, SB)), dma((2, SB)),
            ],
            compiler_params=pltpu.CompilerParams(vmem_limit_bytes=60 * 2**20),
            name="widen",
        )(vector, image)
        return vector, image, ritz

    in_specs = (
        P(("groups", "sector"), None, None, "rep"),
        P(("groups", "sector"), None, None, "rep"),
        P("term", ("groups", "sector"), None, None, None),
        P("term", "sector", "groups", None, "rep"),
        P("term", ("groups", "sector"), None),
    )
    out_specs = (
        P(("groups", "sector"), None, None, "rep"),
        P(("groups", "sector"), None, None, "rep"),
        P("groups"),
    )
    return jax.shard_map(local, mesh=mesh, in_specs=in_specs, out_specs=out_specs, check_vma=False)
```

```python
import functools
import jax
import jax.numpy as jnp
from jax import lax
from jax.experimental import pallas as pl
from jax.experimental.pallas import tpu as pltpu
from jax.sharding import PartitionSpec as P

eps = 1e-06
MESH = pl.DeviceIdType.MESH
f32 = jnp.float32
bf16 = jnp.bfloat16


def loop(low, high, body):
    if high - low <= 16:
        for k in range(low, high):
            body(k)
    else:
        lax.fori_loop(low, high, lambda k, c: (body(k), c)[1], 0)


def pack(sums):
    lane = lax.broadcasted_iota(jnp.int32, (1, 128), 1)
    row = jnp.zeros((1, 128), f32)
    for k, value in enumerate(sums):
        if value.shape != (1, 1):
            value = jnp.sum(value, axis=1, keepdims=True)
        row = row + jnp.where(lane == k, value, 0.0)
    return row


def partial(products):
    total = products[0]
    for other in products[1:]:
        total = total + other
    return jnp.sum(total, axis=0, keepdims=True)


def kernel(
    S, T, R, nj, count,
    v_in, p_in, l_in, r_in, used,
    nv_out, img_out, ritz_out,
    vloc, ploc, vbuf, pbuf, lbuf, rbuf, s0buf, s1buf, imgbuf, s0in, s1in, nvbuf, rows,
    local_sem, vsem, psem, lsem, rsem, row_sem, row_send, v_send, p_send, l_send, r_send,
    out_sem, out_send, ploc_sem, nv_sem,
):
    N = S * T * R
    SB = nj * T * R
    B = lbuf.shape[-1]
    H = B // R
    s, t, r = lax.axis_index("sector"), lax.axis_index("term"), lax.axis_index("rep")
    me = (s * T + t) * R + r

    def device(rank):
        return {"sector": rank // (T * R), "term": lax.rem(rank // R, T), "rep": lax.rem(rank, R)}

    order = [a for a in (S - 1, 1) if 0 < a] if S > 1 else []
    order = list(dict.fromkeys(order + list(range(2, S - 1)))) + [0]
    peers = [(a, b, c) for a in order for b in reversed(range(T)) for c in reversed(range(R))][:-1]

    def each_peer(body):
        if N <= 16:
            for a, b, c in peers:
                body({"sector": lax.rem(s + a, S), "term": lax.rem(t + b, T), "rep": lax.rem(r + c, R)})
        else:
            lax.fori_loop(1, N, lambda k, c: (body(device(lax.rem(me + k, N))), c)[1], 0)

    def first(t2, r2):
        return (t2 * R + r2) * nj

    def half(r2):
        return pl.ds(pl.multiple_of(r2 * H, H), H)

    C = B // 2
    tiles = ((pl.ds(C, C), pl.ds(0, B)), (pl.ds(0, C), pl.ds(0, C)))

    own = pl.ds(first(t, r), nj)
    load = pltpu.make_async_copy(v_in.at[0], vloc, local_sem)
    load.start()
    pltpu.make_async_copy(v_in.at[0, own], vbuf.at[:, :, half(r)], vsem).start()
    pltpu.make_async_copy(p_in.at[0, own], pbuf.at[:, :, half(r)], psem).start()
    for rows_of, lanes_of in tiles:
        pltpu.make_async_copy(
            l_in.at[0, 0, own, rows_of, lanes_of], lbuf.at[t, :, rows_of, lanes_of], lsem
        ).start()

    barrier = pltpu.get_barrier_semaphore()

    def greet(peer):
        pl.semaphore_signal(barrier, inc=1, device_id=peer, device_id_type=MESH)

    each_peer(greet)

    load.wait()
    lane = lax.broadcasted_iota(jnp.int32, (1, 128), 1)
    local_v = [vloc[t * R * nj + k].astype(f32) for k in range(R * nj)]
    row = pack([partial([x * x for x in local_v])])
    for j in range(SB):
        row = row + jnp.where(lane == 8 + j, used[0, 0, j].astype(f32), 0.0)

    def send_row(index, row):
        rows[index, me] = row

        def one(peer):
            pltpu.make_async_remote_copy(
                rows.at[index, me], rows.at[index, me], row_send.at[index], row_sem.at[index],
                device_id=peer, device_id_type=MESH,
            ).start()

        each_peer(one)

    def wait_rows(index):
        some = rows.at[index, pl.ds(0, N - 1)]
        pltpu.make_async_copy(some, some, row_sem.at[index]).wait()
        return rows[index].reshape(N, 128)

    pl.semaphore_wait(barrier, N - 1)
    send_row(0, row)

    p_load = pltpu.make_async_copy(p_in.at[0], ploc, ploc_sem)
    p_load.start()

    def v_copy(k, src, dst, sem, recv):
        r2 = lax.rem(r + k, R)
        return pltpu.make_async_remote_copy(
            src.at[0, pl.ds(first(t, r2), nj)], dst.at[:, :, half(r)], sem.at[k - 1], recv,
            device_id={"sector": s, "term": t, "rep": r2}, device_id_type=MESH,
        )

    def l_copy(k, which):
        t2 = lax.rem(t + k, T)
        rows_of, lanes_of = tiles[which]
        return pltpu.make_async_remote_copy(
            l_in.at[0, 0, pl.ds(first(t2, r), nj), rows_of, lanes_of],
            lbuf.at[t, :, rows_of, lanes_of], l_send.at[k - 1, which], lsem,
            device_id={"sector": s, "term": t2, "rep": r}, device_id_type=MESH,
        )

    owner = s // nj
    owner_t, owner_r, slot = owner // R, lax.rem(owner, R), lax.rem(s, nj)
    mine = jnp.logical_and(owner_t == t, owner_r == r)

    def r_copy(k, rows_of):
        i2 = lax.rem(s + k, S)
        return pltpu.make_async_remote_copy(
            r_in.at[0, 0, i2, rows_of], rbuf.at[t, slot, rows_of, half(r)], r_send.at[k], rsem,
            device_id={"sector": i2, "term": owner_t, "rep": owner_r}, device_id_type=MESH,
        )

    loop(1, R, lambda k: v_copy(k, v_in, vbuf, v_send, vsem).start())
    loop(1, T, lambda k: l_copy(k, 0).start())
    loop(1, T, lambda k: l_copy(k, 1).start())
    def right(rows_of, finish):
        for k in order[:-1]:
            copy = r_copy(k, rows_of)
            copy.wait_send() if finish else copy.start()

        if not finish:

            @pl.when(mine)
            def _():
                pltpu.make_async_copy(
                    r_in.at[0, 0, s, rows_of], rbuf.at[t, slot, rows_of, half(r)], rsem
                ).start()

        @pl.when(jnp.logical_not(mine))
        def _():
            copy = r_copy(0, rows_of)
            copy.wait_send() if finish else copy.start()

    def both_halves(finish):
        pl.when(r == 0)(lambda: right(pl.ds(0, B), finish))
        pl.when(r != 0)(lambda: right(pl.ds(C, C), finish))

    both_halves(False)

    loop(1, R, lambda k: v_copy(k, p_in, pbuf, p_send, psem).start())

    def whole(ref, sem):
        pltpu.make_async_copy(ref, ref, sem).wait()

    m0 = wait_rows(0)
    square = jnp.sum(m0[:, 0:1], axis=0, keepdims=True) / count
    scale = 1.0 / jnp.sqrt(square + eps)
    masks = []
    for t2 in range(T):
        peer_row = rows[0, (s * T + t2) * R + r]
        masks.append([
            jnp.sum(jnp.where(lane == 8 + first(t, r) + q, peer_row, 0.0), axis=1, keepdims=True)
            for q in range(nj)
        ])
    whole(vbuf, vsem)
    v0 = [vbuf[q].astype(f32) * scale for q in range(nj)]
    whole(lbuf.at[:, :, pl.ds(0, 3 * B // 4)], lsem)

    def complete(buf):
        for t2 in range(T):
            for q in range(nj):
                buf[t2, q, 0:C, C:B] = buf[t2, q, C:B, 0:C].T

    complete(lbuf)

    def mix(v):
        result = []
        for q in range(nj):
            rounded = v[q].astype(bf16)
            for t2 in range(T):
                mixed = jnp.dot(lbuf[t2, q], rounded, preferred_element_type=f32)
                result.append((mixed * masks[t2][q]).astype(bf16))
        return result

    def finish(mixed):
        result = []
        for q in range(nj):
            total = None
            for t2 in range(T):
                piece = lax.dot_general(
                    mixed[q * T + t2], rbuf[t2, q], (((1,), (1,)), ((), ())),
                    preferred_element_type=f32,
                )
                total = piece if total is None else total + piece
            result.append(total)
        return result

    def apply_h(v):
        return finish(mix(v))

    def inner(x, y):
        return partial([a * b for a, b in zip(x, y)])

    def lanes(x):
        return jnp.sum(x, axis=1, keepdims=True)

    def columns(m, n):
        return [m[:, k:k + 1] for k in range(n)]

    def add(x):
        return jnp.sum(x, axis=0, keepdims=True) / count

    def out_copy(k, src, dst, which):
        place = lax.rem(t * R + r + k, T * R)
        t2, r2 = place // R, lax.rem(place, R)
        if k == 0:
            return pltpu.make_async_copy(src.at[:, :, half(r2)], dst.at[own], out_sem.at[which])
        return pltpu.make_async_remote_copy(
            src.at[:, :, half(r2)], dst.at[own], out_send.at[which, k - 1], out_sem.at[which],
            device_id={"sector": s, "term": t2, "rep": r2}, device_id_type=MESH,
        )

    sent = ((s0buf, s0in), (s1buf, s1in), (imgbuf, img_out.at[0]))

    def spread(which, value):
        src, dst = sent[which]
        for q in range(nj):
            src[q] = value[q].astype(src.dtype)
        for k in range(T * R):
            out_copy((k + T * R // 2) % (T * R), src, dst, which).start()

    mixed0 = mix(v0)
    whole(pbuf, psem)
    ip = [1.0 / pbuf[q].astype(f32) for q in range(nj)]
    whole(rbuf.at[:, :, pl.ds(0, 3 * B // 4)], rsem)
    complete(rbuf)
    s0 = finish(mixed0)
    n_loc = lanes(inner(v0, v0))
    a_loc = lanes(inner(v0, s0))
    th_loc = a_loc / jnp.maximum(n_loc, 1e-30)
    bb = [a * b for a, b in zip(v0, ip)]
    tt = [(a - th_loc * b) * c for a, b, c in zip(s0, v0, ip)]
    send_row(1, pack([
        n_loc, a_loc, th_loc, inner(v0, tt), inner(v0, bb), inner(tt, tt), inner(tt, bb),
        inner(bb, bb), inner(tt, s0), inner(bb, s0),
    ]))
    spread(0, s0)
    n0, a0, th, vt, vb, t_t, t_b, b_b, ts, bs = columns(wait_rows(1), 10)
    theta = add(a0)
    delta = th - theta
    coef = add(vt + delta * vb)
    length = add(
        t_t + delta * (2.0 * t_b + delta * b_b) - coef * (2.0 * (vt + delta * vb) - coef * n0)
    )
    inv = 1.0 / jnp.sqrt(jnp.maximum(length, 0.0) + eps)
    cross = add(ts + delta * bs - coef * a0) * inv
    d_loc = th_loc - theta
    v1 = [(x + d_loc * y - coef * z) * inv for x, y, z in zip(tt, bb, v0)]

    s1 = apply_h(v1)
    xx = [(x - theta * y - cross * z) * w for x, y, z, w in zip(s0, v0, v1, ip)]
    zz = [x * y for x, y in zip(v1, ip)]
    n1_loc = lanes(inner(v1, v1))
    d1_loc = lanes(inner(v1, s1))
    g_loc = d1_loc / jnp.maximum(n1_loc, 1e-30)
    yy = [(x - cross * y - g_loc * z) * w for x, y, z, w in zip(s1, v0, v1, ip)]
    send_row(2, pack([
        n1_loc, d1_loc, g_loc, inner(v0, v1),
        inner(xx, xx), inner(xx, yy), inner(xx, zz), inner(yy, yy), inner(yy, zz), inner(zz, zz),
        inner(v0, xx), inner(v0, yy), inner(v0, zz), inner(v1, xx), inner(v1, yy), inner(v1, zz),
    ]))
    spread(1, s1)
    (n1, d1, g, o01, xx_, xy_, xz_, yy_, yz_, zz_, ax, ay, az, bx, by, bz) = columns(wait_rows(2), 16)
    diag = add(d1)
    gap = (theta - diag) * 0.5
    lowest = (theta + diag) * 0.5 - jnp.sqrt(gap * gap + cross * cross)
    size = jnp.sqrt(cross * cross + (lowest - theta) * (lowest - theta))
    c0 = cross / size
    c1 = (lowest - theta) / size
    e = c1 * (g - diag)
    f0d = c0 * ax + c1 * ay + e * az
    f1d = c0 * bx + c1 * by + e * bz
    f0 = add(f0d)
    f1 = add(f1d)
    square1 = (
        c0 * c0 * xx_ + c1 * c1 * yy_ + e * e * zz_
        + 2.0 * (c0 * c1 * xy_ + c0 * e * xz_ + c1 * e * yz_)
    )
    length1 = add(
        square1 - 2.0 * (f0 * f0d + f1 * f1d) + f0 * f0 * n0 + f1 * f1 * n1 + 2.0 * f0 * f1 * o01
    )
    inv1 = 1.0 / jnp.sqrt(jnp.maximum(length1, 0.0) + eps)
    e_loc = c1 * (g_loc - diag)
    v2 = []
    for q in range(nj):
        new = (c0 * xx[q] + c1 * yy[q] + e_loc * zz[q] - f0 * v0[q] - f1 * v1[q]) * inv1
        v2.append(new)

    s2 = apply_h(v2)
    spread(2, s2)

    p_load.wait()
    whole(s0in, out_sem.at[0])
    whole(s1in, out_sem.at[1])
    for j in range(SB):
        v0_j = vloc[j].astype(f32) * scale
        ip_j = 1.0 / ploc[j].astype(f32)
        s0_j, s1_j = s0in[j], s1in[j].astype(f32)
        r0_j = s0_j - theta * v0_j
        v1_j = (r0_j * ip_j - coef * v0_j) * inv
        r1_j = c0 * (r0_j - cross * v1_j) + c1 * (s1_j - cross * v0_j - diag * v1_j)
        nvbuf[j] = (r1_j * ip_j - f0 * v0_j - f1 * v1_j) * inv1
    nv_store = pltpu.make_async_copy(nvbuf, nv_out.at[0], nv_sem)
    nv_store.start()
    ritz_out[0] = jnp.sum(lowest)

    for index in range(3):
        some = rows.at[index, pl.ds(0, N - 1)]
        pltpu.make_async_copy(some, some, row_send.at[index]).wait()
    loop(1, R, lambda k: v_copy(k, v_in, vbuf, v_send, vsem).wait_send())
    loop(1, R, lambda k: v_copy(k, p_in, pbuf, p_send, psem).wait_send())
    both_halves(True)
    loop(1, T, lambda k: l_copy(k, 0).wait_send())
    loop(1, T, lambda k: l_copy(k, 1).wait_send())
    for which, (src, dst) in enumerate(sent):
        for k in range(1, T * R):
            out_copy(k, src, dst, which).wait_send()
    whole(img_out.at[0], out_sem.at[2])
    nv_store.wait()


def widen(a_in, b_in, a_out, b_out, a_buf, b_buf, b_wide, load_sem, store_sem):
    sets = ((a_in, a_buf, a_buf, a_out), (b_in, b_buf, b_wide, b_out))
    places = [(w, j) for j in range(a_buf.shape[0]) for w in range(2)]

    def load(w, j):
        return pltpu.make_async_copy(sets[w][0].at[0, j], sets[w][1].at[j], load_sem.at[w, j])

    def store(w, j):
        return pltpu.make_async_copy(sets[w][2].at[j], sets[w][3].at[0, j], store_sem.at[w, j])

    for place in places:
        load(*place).start()
    for w, j in places:
        load(w, j).wait()
        if w == 1:
            b_wide[j] = b_buf[j].astype(f32)
        store(w, j).start()
    for place in places:
        store(*place).wait()


def solution(mesh):
    S, T, R = mesh.shape["sector"], mesh.shape["term"], mesh.shape["rep"]

    def local(start_vector, precond, left_env, right_env, blocks_used):
        SB, B, H = start_vector.shape[1:]
        nj = SB // (T * R)
        N = S * T * R
        count = float(start_vector.size * S * R)
        dma = pltpu.SemaphoreType.DMA
        hbm = pl.BlockSpec(memory_space=pltpu.HBM)
        smem = pl.BlockSpec(memory_space=pltpu.SMEM)
        shape = jax.ShapeDtypeStruct(start_vector.shape, bf16)
        wide = jax.ShapeDtypeStruct(start_vector.shape, f32)
        vector, image, ritz = pl.pallas_call(
            functools.partial(kernel, S, T, R, nj, count),
            out_shape=(wide, shape, jax.ShapeDtypeStruct((1,), f32)),
            in_specs=[hbm, hbm, hbm, hbm, smem],
            out_specs=(hbm, hbm, smem),
            scratch_shapes=[
                pltpu.VMEM((SB, B, H), bf16),
                pltpu.VMEM((SB, B, H), bf16),
                pltpu.VMEM((nj, B, B), bf16),
                pltpu.VMEM((nj, B, B), bf16),
                pltpu.VMEM((T, nj, B, B), bf16),
                pltpu.VMEM((T, nj, B, B), bf16),
                pltpu.VMEM((nj, B, B), f32),
                pltpu.VMEM((nj, B, B), bf16),
                pltpu.VMEM((nj, B, B), bf16),
                pltpu.VMEM((SB, B, H), f32),
                pltpu.VMEM((SB, B, H), bf16),
                pltpu.VMEM((SB, B, H), f32),
                pltpu.VMEM((3, N, 1, 128), f32),
                dma, dma, dma, dma, dma, dma((3,)), dma((3,)), dma((R,)), dma((R,)), dma((T, 2)),
                dma((S,)), dma((3,)), dma((3, T * R)), dma, dma,
            ],
            compiler_params=pltpu.CompilerParams(
                collective_id=0, has_side_effects=True, vmem_limit_bytes=60 * 2**20
            ),
            name="davidson",
        )(start_vector, precond, left_env, right_env, blocks_used)
        vector, image = pl.pallas_call(
            widen,
            out_shape=(wide, wide),
            in_specs=[hbm, hbm],
            out_specs=(hbm, hbm),
            scratch_shapes=[
                pltpu.VMEM((SB, B, H), f32), pltpu.VMEM((SB, B, H), bf16),
                pltpu.VMEM((SB, B, H), f32),
                dma((2, SB)), dma((2, SB)),
            ],
            compiler_params=pltpu.CompilerParams(vmem_limit_bytes=60 * 2**20),
            name="widen",
        )(vector, image)
        return vector, image, ritz

    in_specs = (
        P(("groups", "sector"), None, None, "rep"),
        P(("groups", "sector"), None, None, "rep"),
        P("term", ("groups", "sector"), None, None, None),
        P("term", "sector", "groups", None, "rep"),
        P("term", ("groups", "sector"), None),
    )
    out_specs = (
        P(("groups", "sector"), None, None, "rep"),
        P(("groups", "sector"), None, None, "rep"),
        P("groups"),
    )
    return jax.shard_map(local, mesh=mesh, in_specs=in_specs, out_specs=out_specs, check_vma=False)
```
